512 devices in a mesh: dp: 8 (over x, z_lo), tensor: 64 (over y, z_hi, core).
Axes of the slice: x: 4, y: 8, z: 8 (z_hi: 4, z_lo: 2; z = z_hi * 2 + z_lo), core: 2. Of those that a mesh axis runs over, the one named last changes fastest.
Arguments:
- tokens_b: bfloat16 [512, 8192], P(('dp', 'tensor')), parts along dimension 0, may hold values from -6 to 6
- tokens_a: bfloat16 [512, 8192], P(('dp', 'tensor')), parts along dimension 0, may hold values from -6 to 6
- grad_out_a: bfloat16 [512, 8192], P(('dp', 'tensor')), parts along dimension 0, may hold values from -6 to 6
- gate_weight: bfloat16 [8192, 26624], P(None, 'tensor'), may hold values from -0.0625 to 0.0625
- up_weight: bfloat16 [8192, 26624], P(None, 'tensor'), may hold values from -0.0625 to 0.0625
- down_weight: bfloat16 [26624, 8192], P('tensor'), may hold values from -0.0390625 to 0.0390625
Outputs:
- output_b: bfloat16 [512, 8192], P(('dp', 'tensor')), parts along dimension 0
- grad_in_a: bfloat16 [512, 8192], P(('dp', 'tensor')), parts along dimension 0
The draws below stay inside these ranges and needn't reach their ends.
There are 8 independent parts, one for each index of `dp`. The reference program is written for one: setup_inputs(seed, part) draws one part's arguments, and reference() takes and returns one part's arrays. A program takes and returns all parts, laid end to end along the dimension named above; an argument that names none is the same for every part. Nothing has to cross between parts.
All inputs are finite; a program needn't handle non-finite values.
Results may differ from the reference program's by a relative error of at most 0.0049.
Values may be sent and summed in bfloat16 or wider, within the bound.
A program may use at most 128 MiB of HBM per device.

```python
import jax
import jax.numpy as jnp
from jax import lax

D = 8192
FF = 26624
TOKENS = 64


def levels(stream_key, dims, shards, least, top_value):
    def one(position, shards_of):
        steps = jax.random.uniform(jax.random.fold_in(jax.random.fold_in(stream_key, 6), position), (shards_of,), jnp.float32, least / len(shards), top_value / len(shards))
        return jnp.repeat(jnp.exp(steps), dims[position] // shards_of).reshape((-1,) + (1,) * (len(dims) - position - 1))

    loudness = one(*shards[0])
    for cut in shards[1:]:
        loudness = loudness * one(*cut)
    return loudness


def gaussian(rng, extent, spread, bound, shards=(), dtype=jnp.bfloat16):
    array = spread * jax.random.normal(rng, extent, jnp.float32)
    if shards:
        array = array * levels(rng, extent, shards, -0.22, 0.18)
    return jnp.clip(array, -bound, bound).astype(dtype)


def setup_inputs(seed: int = 0, part: int = 0) -> dict:
    streams_of = jax.random.split(jax.random.key(seed), 7)
    part_keys = jax.random.split(jax.random.fold_in(streams_of[6], part), 7)
    tokens_b = gaussian(part_keys[0], (TOKENS, D), 1.0, 6.0, ((0, 64),))
    tokens_a = gaussian(part_keys[1], (TOKENS, D), 1.0, 6.0, ((0, 64),))
    grad_out_a = gaussian(part_keys[2], (TOKENS, D), 1.0, 6.0, ((0, 64),))
    gate_weight = gaussian(streams_of[3], (D, FF), D ** -0.5, 0.0625, ((1, 64),))
    up_weight = gaussian(streams_of[4], (D, FF), D ** -0.5, 0.0625, ((1, 64),))
    down_weight = gaussian(streams_of[5], (FF, D), FF ** -0.5, 0.0390625, ((0, 64),))
    return {"tokens_b": tokens_b, "tokens_a": tokens_a, "grad_out_a": grad_out_a, "gate_weight": gate_weight, "up_weight": up_weight, "down_weight": down_weight}


def reference(tokens_b, tokens_a, grad_out_a, gate_weight, up_weight, down_weight):
    gate_b = jnp.dot(tokens_b, gate_weight, preferred_element_type=jnp.float32)
    up_b = jnp.dot(tokens_b, up_weight, preferred_element_type=jnp.float32)
    hidden_b = (jax.nn.silu(gate_b) * up_b).astype(jnp.bfloat16)
    output_b = jnp.dot(hidden_b, down_weight, preferred_element_type=jnp.float32).astype(jnp.bfloat16)
    gate_a = jnp.dot(tokens_a, gate_weight, preferred_element_type=jnp.float32)
    up_a = jnp.dot(tokens_a, up_weight, preferred_element_type=jnp.float32)
    contract = (((1,), (1,)), ((), ()))
    grad_hidden = lax.dot_general(grad_out_a, down_weight, contract, preferred_element_type=jnp.float32)
    sigma = jax.nn.sigmoid(gate_a)
    grad_gate = (grad_hidden * up_a * sigma * (1.0 + gate_a * (1.0 - sigma))).astype(jnp.bfloat16)
    grad_up = (grad_hidden * gate_a * sigma).astype(jnp.bfloat16)
    grad_in = lax.dot_general(grad_gate, gate_weight, contract, preferred_element_type=jnp.float32)
    grad_in = grad_in + lax.dot_general(grad_up, up_weight, contract, preferred_element_type=jnp.float32)
    return output_b, grad_in.astype(jnp.bfloat16)
```

```python
import functools

import jax
import jax.numpy as jnp
from jax import lax
from jax.experimental import pallas as pl
from jax.experimental.pallas import tpu as pltpu
from jax.sharding import PartitionSpec as P

MESH = pl.DeviceIdType.MESH
f32, bf16 = jnp.float32, jnp.bfloat16
NT = (((1,), (1,)), ((), ()))
LANES = 128
NY, NZ, NC = 8, 4, 2


def kernel(
    ny, nz, xb, xa, xg, wg_hbm, wu_hbm, wd_hbm, out_b, out_a,
    wg, wu, wd, comm, commg, stage, op_t, op_g, part, psend, precv,
    s1, r1, t1, q1s, q1r, s2, r2, t2, q2s, q2r,
    w_sem, z_s, z_r, ring_s, ring_r, sib_s, sib_r,
    gy_s, gy_r, gz_s, gz_r, gsib_s, gsib_r,
    p_s, p_r, a_s, a_r, b_s, b_r,
):
    d = wg.shape[1]
    rows = d // LANES
    half = rows // 2
    per_core = ny * nz
    tokens = per_core * NC

    t = lax.axis_index("tensor")
    c = lax.rem(t, NC)
    z = lax.rem(lax.div(t, NC), nz)
    y = lax.div(t, NC * nz)

    def at(yy, zz, cc):
        return {"tensor": (yy * nz + zz) * NC + cc}

    def yr(k):
        return lax.rem(y + k, ny)

    def zr(k):
        return lax.rem(z + k, nz)

    sib = at(y, z, 1 - c)
    sent = []

    def send(src, dst, ss, rs, dev):
        cp = pltpu.make_async_remote_copy(
            src_ref=src, dst_ref=dst, send_sem=ss, recv_sem=rs, device_id=dev, device_id_type=MESH
        )
        cp.start()
        sent.append(cp)
        return cp

    loads = [
        pltpu.make_async_copy(h, v, w_sem.at[i])
        for i, (h, v) in enumerate(((wd_hbm, wd), (wg_hbm, wg), (wu_hbm, wu)))
    ]
    for cp in loads:
        cp.start()

    barrier = pltpu.get_barrier_semaphore()
    peers = [at(yr(k), z, c) for k in range(1, ny)] + [at(y, zr(k), c) for k in range(1, nz)] + [sib]
    for dev in peers:
        pl.semaphore_signal(barrier, inc=1, device_id=dev, device_id_type=MESH)

    def own_row(x, dst):
        for s in range(rows):
            stage[s : s + 1, :] = x[0:1, s * LANES : (s + 1) * LANES].astype(f32)
        dst[...] = stage[0:rows, :].astype(bf16)

    zrow = pl.ds(pl.multiple_of(z * rows, rows), rows)
    yrow = pl.ds(pl.multiple_of(y * rows, rows), rows)
    own_row(xg, commg.at[c, z, yrow])
    own_row(xb, comm.at[0, c, y, zrow])
    own_row(xa, comm.at[1, c, y, zrow])
    pl.semaphore_wait(barrier, len(peers))

    gy = []
    zs = [[], []]
    for k in range(1, max(ny, nz)):
        if k < nz:
            for i in range(2):
                ref = comm.at[i, c, y, zrow]
                zs[i].append(send(ref, ref, z_s.at[i, k - 1], z_r.at[i, k - 1], at(y, zr(k), c)))
        if k < ny:
            ref = commg.at[c, z, yrow]
            gy.append(send(ref, ref, gy_s.at[k - 1], gy_r.at[k - 1], at(yr(k), z, c)))

    sibs = [[], []]
    ring = [[[], []], [[], []]]

    def to_sibling(i, k):
        ref = comm.at[i, c, yr(k)]
        sibs[i].append(send(ref, ref, sib_s.at[i, k], sib_r.at[i, k], sib))

    def ring_step(i, way, step):
        k = lax.rem(y + (ny - step if way == 0 else step), ny)
        ref = comm.at[i, c, k]
        dev = at(yr(1 if way == 0 else ny - 1), z, c)
        ring[i][way].append(send(ref, ref, ring_s.at[i, way, step], ring_r.at[i, way, step], dev))

    def steps_of(i, way):
        return ny // 2 - (1 if (i == way) else 0)

    for i in range(2):
        for cp in zs[i]:
            cp.wait_recv()
        for way in range(2):
            ring_step(i, way, 0)
        to_sibling(i, 0)
    for cp in gy:
        cp.wait_recv()
    gz = []
    gsibs = []
    ref = commg.at[c, z]
    for k in range(1, nz):
        gz.append(send(ref, ref, gz_s.at[k - 1], gz_r.at[k - 1], at(y, zr(k), c)))
    gsibs.append(send(ref, ref, gsib_s.at[0], gsib_r.at[0], sib))

    for step in range(ny // 2):
        for i in range(2):
            for way in range(2):
                if step < steps_of(i, way):
                    ring[i][way][step].wait_recv()
                    if step + 1 < steps_of(i, way):
                        ring_step(i, way, step + 1)
                    to_sibling(i, (ny - step - 1) if way == 0 else step + 1)

    for k in range(1, nz):
        gz[k - 1].wait_recv()
        ref = commg.at[c, zr(nz - k)]
        gsibs.append(send(ref, ref, gsib_s.at[k], gsib_r.at[k], sib))

    def to_operand(dst, lo):
        for s in range(rows):
            dst[lo : lo + tokens, s * LANES : (s + 1) * LANES] = stage[
                pl.ds(s, tokens, stride=rows), :
            ].astype(bf16)

    def product(w, v):
        return lax.dot_general(w[...], v, NT, preferred_element_type=f32)

    for i in range(2):
        for cp in sibs[i]:
            cp.wait_recv()
        for cc in range(NC):
            for yy in range(ny):
                lo = (cc * ny + yy) * nz * rows
                stage[lo : lo + nz * rows, :] = comm[i, cc, yy].astype(f32)
        to_operand(op_t, i * tokens)
    loads[1].wait()
    gate = product(wg, op_t[...]).T
    loads[2].wait()
    upper = product(wu, op_t[...]).T
    sigma = jax.nn.sigmoid(gate)
    hidden_b = (gate[:tokens] * sigma[:tokens] * upper[:tokens]).astype(bf16)

    for cp in gsibs:
        cp.wait_recv()
    for cc in range(NC):
        for zz in range(nz):
            for yy in range(ny):
                lo = ((cc * ny + yy) * nz + zz) * rows
                stage[lo : lo + rows, :] = commg[cc, zz, yy * rows : (yy + 1) * rows].astype(f32)
    to_operand(op_g, 0)
    loads[0].wait()
    grad_hidden = product(wd, op_g[...]).T
    gate_a, up_a, sg = gate[tokens:], upper[tokens:], sigma[tokens:]
    grad_gate = (grad_hidden * up_a * sg * (1.0 + gate_a * (1.0 - sg))).astype(bf16)
    grad_up = (grad_hidden * gate_a * sg).astype(bf16)

    width = min(d // 2, 2048)

    def columns(i, h):
        for lo in range(h * (d // 2), (h + 1) * (d // 2), width):
            cut = slice(lo, lo + width)
            if i == 0:
                v = jnp.dot(hidden_b, wd[:, cut], preferred_element_type=f32)
            else:
                v = jnp.dot(grad_gate, wg[:, cut], preferred_element_type=f32)
                v = v + jnp.dot(grad_up, wu[:, cut], preferred_element_type=f32)
            for s in range(width // LANES):
                row = (lo - h * (d // 2)) // LANES + s
                part[i, h, pl.ds(row, tokens, stride=half), :] = v[:, s * LANES : (s + 1) * LANES]

    core_rows = per_core * half

    def pair(i, h):
        lo = pl.multiple_of((1 - c) * core_rows, core_rows)
        psend[i, h] = part[i, h, pl.ds(lo, core_rows), :].astype(bf16)
        return send(psend.at[i, h], precv.at[i, h], p_s.at[i, h], p_r.at[i, h], sib)

    def mine(i, h, lo, n):
        lo = pl.multiple_of(lo, n)
        own = part[i, h, pl.ds(pl.multiple_of(c * core_rows + lo, n), n), :]
        return own + precv[i, h, pl.ds(lo, n), :].astype(f32)

    yb, zb = nz * half, ny * half

    def round_one(i, h, cp):
        cp.wait_recv()
        out = []
        if h == 0:
            for k in range(1, ny):
                s1[i, k - 1] = mine(i, h, yr(k) * yb, yb).astype(bf16)
                out.append(send(s1.at[i, k - 1], r1.at[i, k - 1], a_s.at[i, h, k - 1], a_r.at[i, h, k - 1], at(yr(k), z, c)))
            t1[i] = mine(i, h, y * yb, yb)
        else:
            for k in range(nz):
                for yy in range(ny):
                    v = mine(i, h, (yy * nz + zr(k)) * half, half)
                    if k:
                        s2[i, k - 1, yy * half : (yy + 1) * half, :] = v.astype(bf16)
                    else:
                        t2[i, yy * half : (yy + 1) * half, :] = v
                if k:
                    out.append(send(s2.at[i, k - 1], r2.at[i, k - 1], a_s.at[i, h, k - 1], a_r.at[i, h, k - 1], at(y, zr(k), c)))
        return out

    def round_two(i, h, cps):
        for cp in cps:
            cp.wait_recv()
        out = []
        if h == 0:
            v = t1[i]
            for k in range(ny - 1):
                v = v + r1[i, k].astype(f32)
            t1[i] = v
            for k in range(1, nz):
                q1s[i, k - 1] = t1[i, pl.ds(pl.multiple_of(zr(k) * half, half), half), :].astype(bf16)
                out.append(send(q1s.at[i, k - 1], q1r.at[i, k - 1], b_s.at[i, h, k - 1], b_r.at[i, h, k - 1], at(y, zr(k), c)))
        else:
            v = t2[i]
            for k in range(nz - 1):
                v = v + r2[i, k].astype(f32)
            t2[i] = v
            for k in range(1, ny):
                q2s[i, k - 1] = t2[i, pl.ds(pl.multiple_of(yr(k) * half, half), half), :].astype(bf16)
                out.append(send(q2s.at[i, k - 1], q2r.at[i, k - 1], b_s.at[i, h, k - 1], b_r.at[i, h, k - 1], at(yr(k), z, c)))
        return out

    def finish(i, h, cps):
        for cp in cps:
            cp.wait_recv()
        out = out_b if i == 0 else out_a
        if h == 0:
            v = t1[i, pl.ds(pl.multiple_of(z * half, half), half), :]
            for k in range(nz - 1):
                v = v + q1r[i, k].astype(f32)
        else:
            v = t2[i, pl.ds(pl.multiple_of(y * half, half), half), :]
            for k in range(ny - 1):
                v = v + q2r[i, k].astype(f32)
        out[h * half : (h + 1) * half, :] = v.astype(bf16)

    pairs, ones, twos = {}, {}, {}
    order = [(0, 1), (0, 0), (1, 1), (1, 0)]
    for j, ih in enumerate(order):
        columns(*ih)
        pairs[ih] = pair(*ih)
        if j >= 1:
            ones[order[j - 1]] = round_one(*order[j - 1], pairs[order[j - 1]])
    ones[order[-1]] = round_one(*order[-1], pairs[order[-1]])
    for ih in order:
        twos[ih] = round_two(*ih, ones[ih])
    for ih in order:
        finish(*ih, twos[ih])
    for cp in sent:
        cp.wait_send()


def local(ny, nz, tokens_b, tokens_a, grad_out_a, gate_weight, up_weight, down_weight):
    h, d = down_weight.shape
    rows = d // LANES
    half = rows // 2
    per_core = ny * nz
    tokens = per_core * NC
    vmem, dma = pltpu.VMEM, pltpu.SemaphoreType.DMA
    row = jax.ShapeDtypeStruct((rows, LANES), bf16)
    in_vmem, anywhere = pl.BlockSpec(memory_space=vmem), pl.BlockSpec(memory_space=pl.ANY)
    output_b, grad_in = pl.pallas_call(
        functools.partial(kernel, ny, nz),
        out_shape=(row, row),
        in_specs=[in_vmem] * 3 + [anywhere] * 3,
        out_specs=(in_vmem, in_vmem),
        scratch_shapes=[
            vmem((h, d), bf16),
            vmem((h, d), bf16),
            vmem((h, d), bf16),
            vmem((2, NC, ny, nz * rows, LANES), bf16),
            vmem((NC, nz, ny * rows, LANES), bf16),
            vmem((tokens * rows, LANES), f32),
            vmem((2 * tokens, d), bf16),
            vmem((tokens, d), bf16),
            vmem((2, 2, tokens * half, LANES), f32),
            vmem((2, 2, per_core * half, LANES), bf16),
            vmem((2, 2, per_core * half, LANES), bf16),
            vmem((2, ny - 1, nz * half, LANES), bf16),
            vmem((2, ny - 1, nz * half, LANES), bf16),
            vmem((2, nz * half, LANES), f32),
            vmem((2, nz - 1, half, LANES), bf16),
            vmem((2, nz - 1, half, LANES), bf16),
            vmem((2, nz - 1, ny * half, LANES), bf16),
            vmem((2, nz - 1, ny * half, LANES), bf16),
            vmem((2, ny * half, LANES), f32),
            vmem((2, ny - 1, half, LANES), bf16),
            vmem((2, ny - 1, half, LANES), bf16),
            dma((3,)),
            dma((2, nz - 1)),
            dma((2, nz - 1)),
            dma((2, 2, ny // 2)),
            dma((2, 2, ny // 2)),
            dma((2, ny)),
            dma((2, ny)),
            dma((ny - 1,)),
            dma((ny - 1,)),
            dma((nz - 1,)),
            dma((nz - 1,)),
            dma((nz,)),
            dma((nz,)),
            dma((2, 2)),
            dma((2, 2)),
            dma((2, 2, ny - 1)),
            dma((2, 2, ny - 1)),
            dma((2, 2, ny - 1)),
            dma((2, 2, ny - 1)),
        ],
        compiler_params=pltpu.CompilerParams(
            collective_id=0, has_side_effects=True, vmem_limit_bytes=60 * 2**20
        ),
        cost_estimate=pl.CostEstimate(flops=2 * 8 * tokens * d * h, bytes_accessed=6 * d * h, transcendentals=0),
        name="swiglu",
    )(tokens_b, tokens_a, grad_out_a, gate_weight.T, up_weight.T, down_weight)
    return output_b.reshape(1, d), grad_in.reshape(1, d)


def solution(mesh, ny=NY, nz=NZ):
    row, column = P(("dp", "tensor"), None), P(None, "tensor")
    return jax.shard_map(
        functools.partial(local, ny, nz),
        mesh=mesh,
        in_specs=(row, row, row, column, column, P("tensor", None)),
        out_specs=(row, row),
        check_vma=False,
    )
```

```python
import functools

import jax
import jax.numpy as jnp
from jax import lax
from jax.experimental import pallas as pl
from jax.experimental.pallas import tpu as pltpu
from jax.sharding import PartitionSpec as P

def firsts(n):
    return [2, -2, 1, -1] if n == 8 else [1, -1] if n == 4 else [1]


def seconds(n):
    return [2, -2] if n == 8 else []


def far_first(n):
    return sorted(range(1, n), key=lambda k: -min(k, n - k))


MESH = pl.DeviceIdType.MESH
f32, bf16 = jnp.float32, jnp.bfloat16
NT = (((1,), (1,)), ((), ()))
LANES = 128
PARTS = 4
NY, NZ, NC = 8, 4, 2


def kernel(
    ny, nz, xb, xa, xg, wg_hbm, wu_hbm, wd_hbm, out_b, out_a,
    wg, wu, wd, comm, commg, stage, op_t, op_g, part, psend, precv,
    s1, r1, t1, q1s, q1r, s2, r2, t2, q2s, q2r, w_sem, s_sem, r_sem,
):
    d = wg.shape[1]
    rows = d // LANES
    fine = rows // PARTS
    per_core = ny * nz
    tokens = per_core * NC

    t = lax.axis_index("tensor")
    c = lax.rem(t, NC)
    z = lax.rem(lax.div(t, NC), nz)
    y = lax.div(t, NC * nz)

    def at(yy, zz, cc):
        return {"tensor": (yy * nz + zz) * NC + cc}

    def yr(k):
        return lax.rem(y + k + ny, ny)

    def zr(k):
        return lax.rem(z + k + nz, nz)

    sib = at(y, z, 1 - c)
    sent = []

    def send(src, dst, dev):
        n = len(sent)
        cp = pltpu.make_async_remote_copy(
            src_ref=src, dst_ref=dst, send_sem=s_sem.at[n], recv_sem=r_sem.at[n], device_id=dev, device_id_type=MESH
        )
        cp.start()
        sent.append(cp)
        return cp

    loads = [
        pltpu.make_async_copy(h, v, w_sem.at[i])
        for i, (h, v) in enumerate(((wd_hbm, wd), (wg_hbm, wg), (wu_hbm, wu)))
    ]
    for cp in loads:
        cp.start()

    barrier = pltpu.get_barrier_semaphore()
    peers = [at(yr(k), z, c) for k in range(1, ny)] + [at(y, zr(k), c) for k in range(1, nz)] + [sib]
    for dev in peers:
        pl.semaphore_signal(barrier, inc=1, device_id=dev, device_id_type=MESH)

    def own_row(x, dst):
        for s in range(rows):
            stage[s : s + 1, :] = x[0:1, s * LANES : (s + 1) * LANES].astype(f32)
        dst[...] = stage[0:rows, :].astype(bf16)

    def place(k, n):
        return pl.ds(pl.multiple_of(k * n, n), n)

    own_row(xb, comm.at[c, y, place(2 * z, rows)])
    own_row(xa, comm.at[c, y, place(2 * z + 1, rows)])
    own_row(xg, commg.at[c, z, place(y, rows)])
    pl.semaphore_wait(barrier, len(peers))

    far_y, far_z = far_first(ny), far_first(nz)

    class Tokens:
        def __init__(self):
            self.along_z, self.near, self.far, self.shared = {}, {}, {}, []

        def unit(self, ky, dz):
            return c, ky, place(zr(dz), 2 * rows)

        def go(self, ref, dev):
            return send(ref, ref, dev)

        def share(self, ky, dz):
            self.shared.append(self.go(comm.at[self.unit(ky, dz)], sib))

        def start(self):
            for k in far_z:
                self.along_z[k] = self.go(comm.at[self.unit(y, 0)], at(y, zr(k), c))

        def first(self, dz):
            if dz:
                self.along_z[(nz - dz) % nz].wait_recv()
            for k in firsts(ny):
                self.near[dz, k] = self.go(comm.at[self.unit(y, dz)], at(yr(k), z, c))
            self.share(y, dz)

        def second(self, dz):
            for k in seconds(ny):
                self.near[dz, k].wait_recv()
                one = place(2 * zr(dz) + (0 if k > 0 else 1), rows)
                self.far[dz, 2 * k] = self.go(comm.at[c, yr(-k), one], at(yr(k), z, c))
                self.far[dz, 3 * k // 2] = self.go(comm.at[self.unit(yr(-k), dz)], at(yr(k // 2), z, c))
                self.share(yr(-k), dz)

        def finish(self, dz):
            for k in firsts(ny):
                if k not in seconds(ny):
                    self.near[dz, k].wait_recv()
                    self.share(yr(-k), dz)
            for k in seconds(ny):
                self.far[dz, 3 * k // 2].wait_recv()
                self.share(yr(-3 * k // 2), dz)
            if seconds(ny):
                self.far[dz, 4].wait_recv()
                self.far[dz, -4].wait_recv()
                self.share(yr(4), dz)

        def to_operand(self):
            for cp in self.shared:
                cp.wait_recv()
            for cc in range(NC):
                for yy in range(ny):
                    for j in range(2 * nz):
                        lo = ((j % 2 * NC + cc) * ny + yy) * nz * rows + j // 2 * rows
                        stage[lo : lo + rows, :] = comm[cc, yy, j * rows : (j + 1) * rows].astype(f32)
            to_operand(op_t, 2 * tokens)

    class Cotangents:
        def __init__(self):
            self.along_y, self.up, self.down, self.shared = [], [], [], []

        def piece(self, k, p):
            n = ny * rows // 2
            return commg.at[c, k, pl.ds(p * n, n)]

        def go(self, k, p, dz):
            ref = self.piece(k, p)
            return send(ref, ref, at(y, zr(dz), c))

        def share(self, k, p):
            ref = self.piece(k, p)
            self.shared.append(send(ref, ref, sib))

        def start(self):
            for k in far_y:
                ref = commg.at[c, z, place(y, rows)]
                self.along_y.append(send(ref, ref, at(yr(k), z, c)))

        def first(self):
            for cp in self.along_y:
                cp.wait_recv()
            for p in range(2):
                self.up.append(self.go(z, p, 1))
                self.down.append(self.go(z, 1 - p, -1))
            for p in range(2):
                self.share(z, p)

        def second(self):
            self.up[0].wait_recv()
            self.up.append(self.go(zr(-1), 0, 1))
            self.share(zr(-1), 0)
            self.down[0].wait_recv()
            self.down.append(self.go(zr(1), 1, -1))
            self.share(zr(1), 1)

        def finish(self):
            self.up[1].wait_recv()
            self.share(zr(-1), 1)
            self.down[1].wait_recv()
            self.share(zr(1), 0)
            self.up[2].wait_recv()
            self.share(zr(2), 0)
            self.down[2].wait_recv()
            self.share(zr(2), 1)

        def to_operand(self):
            for cp in self.shared:
                cp.wait_recv()
            for cc in range(NC):
                for zz in range(nz):
                    for yy in range(ny):
                        lo = ((cc * ny + yy) * nz + zz) * rows
                        stage[lo : lo + rows, :] = commg[cc, zz, yy * rows : (yy + 1) * rows].astype(f32)
            to_operand(op_g, tokens)

    def to_operand(op, n):
        for s in range(rows):
            op[:, s * LANES : (s + 1) * LANES] = stage[pl.ds(s, n, stride=rows), :].astype(bf16)

    def product(w, op):
        return lax.dot_general(op[...], w[...], NT, preferred_element_type=f32)

    width = d // PARTS
    both = 2 * fine
    core_rows = per_core * both
    yb = nz * both

    class Part:
        def __init__(self, q, left_b, left_a):
            self.q, self.b, self.z_first = q, q // 2, q % 2 == 0
            for i, pairs_of in enumerate((left_b, left_a)):
                v = sum(
                    jnp.dot(left, w[:, q * width : (q + 1) * width], preferred_element_type=f32)
                    for left, w in pairs_of
                )
                for s in range(fine):
                    part[q, pl.ds(i * fine + s, tokens, stride=both), :] = v[:, s * LANES : (s + 1) * LANES]
            psend[q] = part[q, place(1 - c, core_rows), :].astype(bf16)
            self.pair = send(psend.at[q], precv.at[q], sib)

        def mine(self, lo, n):
            lo = pl.multiple_of(lo, n)
            own = part[self.q, pl.ds(pl.multiple_of(c * core_rows + lo, n), n)]
            return own + precv[self.q, pl.ds(lo, n)].astype(f32)

        def one(self):
            self.pair.wait_recv()
            self.cps = []
            b = self.b
            if self.z_first:
                for k in far_z + [0]:
                    for yy in range(ny):
                        v = self.mine((yy * nz + zr(k)) * both, both)
                        if k:
                            s2[b, k - 1, yy * both : (yy + 1) * both] = v.astype(bf16)
                        else:
                            t2[b, yy * both : (yy + 1) * both] = v
                    if k:
                        self.cps.append(send(s2.at[b, k - 1], r2.at[b, k - 1], at(y, zr(k), c)))
            else:
                for k in far_y:
                    s1[b, k - 1] = self.mine(yr(k) * yb, yb).astype(bf16)
                    self.cps.append(send(s1.at[b, k - 1], r1.at[b, k - 1], at(yr(k), z, c)))
                t1[b] = self.mine(y * yb, yb)

        def two(self):
            for cp in self.cps:
                cp.wait_recv()
            self.cps = []
            b = self.b
            if self.z_first:
                v = t2[b]
                for k in range(nz - 1):
                    v = v + r2[b, k].astype(f32)
                t2[b] = v
                for k in far_y:
                    q2s[b, k - 1] = t2[b, place(yr(k), both)].astype(bf16)
                    self.cps.append(send(q2s.at[b, k - 1], q2r.at[b, k - 1], at(yr(k), z, c)))
            else:
                v = t1[b]
                for k in range(ny - 1):
                    v = v + r1[b, k].astype(f32)
                t1[b] = v
                for k in far_z:
                    q1s[b, k - 1] = t1[b, place(zr(k), both)].astype(bf16)
                    self.cps.append(send(q1s.at[b, k - 1], q1r.at[b, k - 1], at(y, zr(k), c)))

        def finish(self):
            for cp in self.cps:
                cp.wait_recv()
            b = self.b
            if self.z_first:
                v = t2[b, place(y, both)]
                for k in range(ny - 1):
                    v = v + q2r[b, k].astype(f32)
            else:
                v = t1[b, place(z, both)]
                for k in range(nz - 1):
                    v = v + q1r[b, k].astype(f32)
            lo = self.q * fine
            out_b[lo : lo + fine, :] = v[:fine].astype(bf16)
            out_a[lo : lo + fine, :] = v[fine:].astype(bf16)

    tt, tg = Tokens(), Cotangents()
    tt.start()
    tg.start()
    tt.first(0)
    tt.first(-1)
    tt.first(1)
    tt.second(0)
    tt.first(2)
    tg.first()
    tt.second(-1)
    tt.second(1)
    tg.second()
    tt.second(2)
    for dz in (0, -1, 1):
        tt.finish(dz)
    tg.finish()
    tt.finish(2)

    tg.to_operand()
    loads[0].wait()
    grad_hidden = product(wd, op_g)
    tt.to_operand()
    loads[1].wait()
    gate = product(wg, op_t)
    loads[2].wait()
    upper = product(wu, op_t)
    sigma = jax.nn.sigmoid(gate)
    hidden_b = (gate[:tokens] * sigma[:tokens] * upper[:tokens]).astype(bf16)
    gate, upper, sigma = gate[tokens:], upper[tokens:], sigma[tokens:]
    grad_gate = (grad_hidden * upper * sigma * (1.0 + gate * (1.0 - sigma))).astype(bf16)
    grad_up = (grad_hidden * gate * sigma).astype(bf16)
    left_b, left_a = [(hidden_b, wd)], [(grad_gate, wg), (grad_up, wu)]
    parts = []
    for q in range(PARTS):
        parts.append(Part(q, left_b, left_a))
        if q:
            parts[q - 1].one()
    parts[-1].one()
    for p in parts:
        p.two()
    for p in parts:
        p.finish()
    for cp in sent:
        cp.wait_send()


def local(ny, nz, tokens_b, tokens_a, grad_out_a, gate_weight, up_weight, down_weight):
    h, d = down_weight.shape
    rows = d // LANES
    both = 2 * (rows // PARTS)
    per_core = ny * nz
    tokens = per_core * NC
    vmem, dma = pltpu.VMEM, pltpu.SemaphoreType.DMA
    row = jax.ShapeDtypeStruct((rows, LANES), bf16)
    in_vmem, anywhere = pl.BlockSpec(memory_space=vmem), pl.BlockSpec(memory_space=pl.ANY)
    output_b, grad_in = pl.pallas_call(
        functools.partial(kernel, ny, nz),
        out_shape=(row, row),
        in_specs=[in_vmem] * 3 + [anywhere] * 3,
        out_specs=(in_vmem, in_vmem),
        scratch_shapes=[
            vmem((h, d), bf16),
            vmem((h, d), bf16),
            vmem((h, d), bf16),
            vmem((NC, ny, 2 * nz * rows, LANES), bf16),
            vmem((NC, nz, ny * rows, LANES), bf16),
            vmem((2 * tokens * rows, LANES), f32),
            vmem((2 * tokens, d), bf16),
            vmem((tokens, d), bf16),
            vmem((PARTS, tokens * both, LANES), f32),
            vmem((PARTS, per_core * both, LANES), bf16),
            vmem((PARTS, per_core * both, LANES), bf16),
            vmem((2, ny - 1, nz * both, LANES), bf16),
            vmem((2, ny - 1, nz * both, LANES), bf16),
            vmem((2, nz * both, LANES), f32),
            vmem((2, nz - 1, both, LANES), bf16),
            vmem((2, nz - 1, both, LANES), bf16),
            vmem((2, nz - 1, ny * both, LANES), bf16),
            vmem((2, nz - 1, ny * both, LANES), bf16),
            vmem((2, ny * both, LANES), f32),
            vmem((2, ny - 1, both, LANES), bf16),
            vmem((2, ny - 1, both, LANES), bf16),
            dma((3,)),
            dma((160,)),
            dma((160,)),
        ],
        compiler_params=pltpu.CompilerParams(
            collective_id=0, has_side_effects=True, vmem_limit_bytes=60 * 2**20
        ),
        cost_estimate=pl.CostEstimate(flops=2 * 8 * tokens * d * h, bytes_accessed=6 * d * h, transcendentals=0),
        name="swiglu",
    )(tokens_b, tokens_a, grad_out_a, gate_weight.T, up_weight.T, down_weight)
    return output_b.reshape(1, d), grad_in.reshape(1, d)


def solution(mesh, ny=NY, nz=NZ):
    row, column = P(("dp", "tensor"), None), P(None, "tensor")
    return jax.shard_map(
        functools.partial(local, ny, nz),
        mesh=mesh,
        in_specs=(row, row, row, column, column, P("tensor", None)),
        out_specs=(row, row),
        check_vma=False,
    )
```

```python
import functools

import jax
import jax.numpy as jnp
from jax import lax
from jax.experimental import pallas as pl
from jax.experimental.pallas import tpu as pltpu
from jax.sharding import PartitionSpec as P

def firsts(n):
    return [2, -2, 1, -1] if n == 8 else [1, -1] if n == 4 else [1]


def seconds(n):
    return [2, -2] if n == 8 else []


def far_first(n):
    return sorted(range(1, n), key=lambda k: -min(k, n - k))


MESH = pl.DeviceIdType.MESH
f32, bf16 = jnp.float32, jnp.bfloat16
NT = (((1,), (1,)), ((), ()))
LANES = 128
PARTS = 4
NY, NZ, NC = 8, 4, 2


def kernel(
    ny, nz, xb, xa, xg, wg_hbm, wu_hbm, wd_hbm, out_b, out_a,
    wg, wu, wd, comm, commg, stage, op_t, op_g, part, psend, precv,
    s1, r1, t1, q1s, q1r, s2, r2, t2, q2s, q2r, w_sem, s_sem, r_sem,
):
    d = wg.shape[1]
    rows = d // LANES
    fine = rows // PARTS
    per_core = ny * nz
    tokens = per_core * NC

    t = lax.axis_index("tensor")
    c = lax.rem(t, NC)
    z = lax.rem(lax.div(t, NC), nz)
    y = lax.div(t, NC * nz)

    def at(yy, zz, cc):
        return {"tensor": (yy * nz + zz) * NC + cc}

    def yr(k):
        return lax.rem(y + k + ny, ny)

    def zr(k):
        return lax.rem(z + k + nz, nz)

    sib = at(y, z, 1 - c)
    sent = []

    def send(src, dst, dev):
        n = len(sent)
        cp = pltpu.make_async_remote_copy(
            src_ref=src, dst_ref=dst, send_sem=s_sem.at[n], recv_sem=r_sem.at[n], device_id=dev, device_id_type=MESH
        )
        cp.start()
        sent.append(cp)
        return cp

    loads = [
        pltpu.make_async_copy(h, v, w_sem.at[i])
        for i, (h, v) in enumerate(((wg_hbm, wg), (wu_hbm, wu), (wd_hbm, wd)))
    ]
    for cp in loads:
        cp.start()

    barrier = pltpu.get_barrier_semaphore()
    peers = [at(yr(k), z, c) for k in range(1, ny)] + [at(y, zr(k), c) for k in range(1, nz)] + [sib]
    for dev in peers:
        pl.semaphore_signal(barrier, inc=1, device_id=dev, device_id_type=MESH)

    def own_row(x, dst):
        for s in range(rows):
            stage[s : s + 1, :] = x[0:1, s * LANES : (s + 1) * LANES].astype(f32)
        dst[...] = stage[0:rows, :].astype(bf16)

    def place(k, n):
        return pl.ds(pl.multiple_of(k * n, n), n)

    own_row(xb, comm.at[c, y, place(2 * z, rows)])
    own_row(xa, comm.at[c, y, place(2 * z + 1, rows)])
    own_row(xg, commg.at[c, z, place(y, rows)])
    pl.semaphore_wait(barrier, len(peers))

    far_y, far_z = far_first(ny), far_first(nz)

    class Tokens:
        def __init__(self):
            self.along_z, self.near, self.far, self.shared = {}, {}, {}, []

        def unit(self, ky, dz):
            return c, ky, place(zr(dz), 2 * rows)

        def go(self, ref, dev):
            return send(ref, ref, dev)

        def share(self, ky, dz):
            self.shared.append(self.go(comm.at[self.unit(ky, dz)], sib))

        def start(self):
            for k in far_z:
                self.along_z[k] = self.go(comm.at[self.unit(y, 0)], at(y, zr(k), c))

        def first(self, dz):
            if dz:
                self.along_z[(nz - dz) % nz].wait_recv()
            for k in firsts(ny):
                self.near[dz, k] = self.go(comm.at[self.unit(y, dz)], at(yr(k), z, c))
            self.share(y, dz)

        def second(self, dz):
            for k in seconds(ny):
                self.near[dz, k].wait_recv()
                one = place(2 * zr(dz) + (0 if k > 0 else 1), rows)
                self.far[dz, 2 * k] = self.go(comm.at[c, yr(-k), one], at(yr(k), z, c))
                self.far[dz, 3 * k // 2] = self.go(comm.at[self.unit(yr(-k), dz)], at(yr(k // 2), z, c))
                self.share(yr(-k), dz)

        def finish(self, dz):
            for k in firsts(ny):
                if k not in seconds(ny):
                    self.near[dz, k].wait_recv()
                    self.share(yr(-k), dz)
            for k in seconds(ny):
                self.far[dz, 3 * k // 2].wait_recv()
                self.share(yr(-3 * k // 2), dz)
            if seconds(ny):
                self.far[dz, 4].wait_recv()
                self.far[dz, -4].wait_recv()
                self.share(yr(4), dz)

        def to_operand(self):
            for cp in self.shared:
                cp.wait_recv()
            for cc in range(NC):
                for yy in range(ny):
                    for j in range(2 * nz):
                        lo = ((j % 2 * NC + cc) * ny + yy) * nz * rows + j // 2 * rows
                        stage[lo : lo + rows, :] = comm[cc, yy, j * rows : (j + 1) * rows].astype(f32)
            to_operand(op_t, 2 * tokens)

    class Cotangents:
        def __init__(self):
            self.along_y, self.up, self.down, self.shared = [], [], [], []

        def piece(self, k, p):
            n = ny * rows // 2
            return commg.at[c, k, pl.ds(p * n, n)]

        def go(self, k, p, dz):
            ref = self.piece(k, p)
            return send(ref, ref, at(y, zr(dz), c))

        def share(self, k, p):
            ref = self.piece(k, p)
            self.shared.append(send(ref, ref, sib))

        def start(self):
            for k in far_y:
                ref = commg.at[c, z, place(y, rows)]
                self.along_y.append(send(ref, ref, at(yr(k), z, c)))

        def first(self):
            for cp in self.along_y:
                cp.wait_recv()
            for p in range(2):
                self.up.append(self.go(z, p, 1))
                self.down.append(self.go(z, 1 - p, -1))
            for p in range(2):
                self.share(z, p)

        def second(self):
            self.up[0].wait_recv()
            self.up.append(self.go(zr(-1), 0, 1))
            self.share(zr(-1), 0)
            self.down[0].wait_recv()
            self.down.append(self.go(zr(1), 1, -1))
            self.share(zr(1), 1)

        def finish(self):
            self.up[1].wait_recv()
            self.share(zr(-1), 1)
            self.down[1].wait_recv()
            self.share(zr(1), 0)
            self.up[2].wait_recv()
            self.share(zr(2), 0)
            self.down[2].wait_recv()
            self.share(zr(2), 1)

        def to_operand(self):
            for cp in self.shared:
                cp.wait_recv()
            for cc in range(NC):
                for zz in range(nz):
                    for yy in range(ny):
                        lo = ((cc * ny + yy) * nz + zz) * rows
                        stage[lo : lo + rows, :] = commg[cc, zz, yy * rows : (yy + 1) * rows].astype(f32)
            to_operand(op_g, tokens)

    def to_operand(op, n):
        for s in range(rows):
            op[:, s * LANES : (s + 1) * LANES] = stage[pl.ds(s, n, stride=rows), :].astype(bf16)

    def product(w, op):
        return lax.dot_general(op[...], w[...], NT, preferred_element_type=f32)

    width = d // PARTS
    core_rows = per_core * fine
    yb = nz * fine

    class Part:
        def __init__(self, i, q, pairs_of):
            self.at, self.buf, self.z_first = (i, q), (i, q // 2), q % 2 == 0
            v = sum(
                jnp.dot(left, w[:, q * width : (q + 1) * width], preferred_element_type=f32) for left, w in pairs_of
            )
            for s in range(fine):
                part[i, q, pl.ds(s, tokens, stride=fine), :] = v[:, s * LANES : (s + 1) * LANES]
            psend[i, q] = part[i, q, place(1 - c, core_rows), :].astype(bf16)
            self.pair = send(psend.at[i, q], precv.at[i, q], sib)

        def mine(self, lo, n):
            lo = pl.multiple_of(lo, n)
            own = part[(*self.at, pl.ds(pl.multiple_of(c * core_rows + lo, n), n))]
            return own + precv[(*self.at, pl.ds(lo, n))].astype(f32)

        def one(self):
            self.pair.wait_recv()
            self.cps = []
            b = self.buf
            if self.z_first:
                for k in far_z + [0]:
                    for yy in range(ny):
                        v = self.mine((yy * nz + zr(k)) * fine, fine)
                        if k:
                            s2[(*b, k - 1, slice(yy * fine, (yy + 1) * fine))] = v.astype(bf16)
                        else:
                            t2[(*b, slice(yy * fine, (yy + 1) * fine))] = v
                    if k:
                        self.cps.append(send(s2.at[(*b, k - 1)], r2.at[(*b, k - 1)], at(y, zr(k), c)))
            else:
                for k in far_y:
                    s1[(*b, k - 1)] = self.mine(yr(k) * yb, yb).astype(bf16)
                    self.cps.append(send(s1.at[(*b, k - 1)], r1.at[(*b, k - 1)], at(yr(k), z, c)))
                t1[b] = self.mine(y * yb, yb)

        def two(self):
            for cp in self.cps:
                cp.wait_recv()
            self.cps = []
            b = self.buf
            if self.z_first:
                v = t2[b]
                for k in range(nz - 1):
                    v = v + r2[(*b, k)].astype(f32)
                t2[b] = v
                for k in far_y:
                    q2s[(*b, k - 1)] = t2[(*b, place(yr(k), fine))].astype(bf16)
                    self.cps.append(send(q2s.at[(*b, k - 1)], q2r.at[(*b, k - 1)], at(yr(k), z, c)))
            else:
                v = t1[b]
                for k in range(ny - 1):
                    v = v + r1[(*b, k)].astype(f32)
                t1[b] = v
                for k in far_z:
                    q1s[(*b, k - 1)] = t1[(*b, place(zr(k), fine))].astype(bf16)
                    self.cps.append(send(q1s.at[(*b, k - 1)], q1r.at[(*b, k - 1)], at(y, zr(k), c)))

        def finish(self):
            for cp in self.cps:
                cp.wait_recv()
            b = self.buf
            if self.z_first:
                v = t2[(*b, place(y, fine))]
                for k in range(ny - 1):
                    v = v + q2r[(*b, k)].astype(f32)
            else:
                v = t1[(*b, place(z, fine))]
                for k in range(nz - 1):
                    v = v + q1r[(*b, k)].astype(f32)
            i, q = self.at
            (out_b, out_a)[i][q * fine : (q + 1) * fine, :] = v.astype(bf16)

    tt, tg = Tokens(), Cotangents()
    tt.start()
    tg.start()
    tt.first(0)
    tt.first(-1)
    tt.first(1)
    tt.first(2)
    tt.second(0)
    tg.first()
    tt.second(-1)
    tt.second(1)
    tg.second()
    tt.second(2)
    for dz in (0, -1, 1):
        tt.finish(dz)
    tg.finish()
    tt.finish(2)

    tt.to_operand()
    loads[0].wait()
    gate = product(wg, op_t)
    loads[1].wait()
    upper = product(wu, op_t)
    sigma = jax.nn.sigmoid(gate)
    hidden_b = (gate[:tokens] * sigma[:tokens] * upper[:tokens]).astype(bf16)
    gate, upper, sigma = gate[tokens:], upper[tokens:], sigma[tokens:]
    loads[2].wait()
    parts_b = [Part(0, q, [(hidden_b, wd)]) for q in range(PARTS)]
    parts_b[0].one()
    parts_b[1].one()
    tg.to_operand()
    parts_b[2].one()
    parts_b[3].one()
    grad_hidden = product(wd, op_g)
    grad_gate = (grad_hidden * upper * sigma * (1.0 + gate * (1.0 - sigma))).astype(bf16)
    grad_up = (grad_hidden * gate * sigma).astype(bf16)
    left_a = [(grad_gate, wg), (grad_up, wu)]
    parts_a = []
    for q in range(PARTS):
        parts_a.append(Part(1, q, left_a))
        if q:
            parts_a[q - 1].one()
    parts_a[-1].one()
    for p in parts_b + parts_a:
        p.two()
    for p in parts_b + parts_a:
        p.finish()
    for cp in sent:
        cp.wait_send()


def local(ny, nz, tokens_b, tokens_a, grad_out_a, gate_weight, up_weight, down_weight):
    h, d = down_weight.shape
    rows = d // LANES
    fine = rows // PARTS
    per_core = ny * nz
    tokens = per_core * NC
    vmem, dma = pltpu.VMEM, pltpu.SemaphoreType.DMA
    row = jax.ShapeDtypeStruct((rows, LANES), bf16)
    in_vmem, anywhere = pl.BlockSpec(memory_space=vmem), pl.BlockSpec(memory_space=pl.ANY)
    output_b, grad_in = pl.pallas_call(
        functools.partial(kernel, ny, nz),
        out_shape=(row, row),
        in_specs=[in_vmem] * 3 + [anywhere] * 3,
        out_specs=(in_vmem, in_vmem),
        scratch_shapes=[
            vmem((h, d), bf16),
            vmem((h, d), bf16),
            vmem((h, d), bf16),
            vmem((NC, ny, 2 * nz * rows, LANES), bf16),
            vmem((NC, nz, ny * rows, LANES), bf16),
            vmem((2 * tokens * rows, LANES), f32),
            vmem((2 * tokens, d), bf16),
            vmem((tokens, d), bf16),
            vmem((2, PARTS, tokens * fine, LANES), f32),
            vmem((2, PARTS, per_core * fine, LANES), bf16),
            vmem((2, PARTS, per_core * fine, LANES), bf16),
            vmem((2, 2, ny - 1, nz * fine, LANES), bf16),
            vmem((2, 2, ny - 1, nz * fine, LANES), bf16),
            vmem((2, 2, nz * fine, LANES), f32),
            vmem((2, 2, nz - 1, fine, LANES), bf16),
            vmem((2, 2, nz - 1, fine, LANES), bf16),
            vmem((2, 2, nz - 1, ny * fine, LANES), bf16),
            vmem((2, 2, nz - 1, ny * fine, LANES), bf16),
            vmem((2, 2, ny * fine, LANES), f32),
            vmem((2, 2, ny - 1, fine, LANES), bf16),
            vmem((2, 2, ny - 1, fine, LANES), bf16),
            dma((3,)),
            dma((192,)),
            dma((192,)),
        ],
        compiler_params=pltpu.CompilerParams(
            collective_id=0, has_side_effects=True, vmem_limit_bytes=60 * 2**20
        ),
        cost_estimate=pl.CostEstimate(flops=2 * 8 * tokens * d * h, bytes_accessed=6 * d * h, transcendentals=0),
        name="swiglu",
    )(tokens_b, tokens_a, grad_out_a, gate_weight.T, up_weight.T, down_weight)
    return output_b.reshape(1, d), grad_in.reshape(1, d)


def solution(mesh, ny=NY, nz=NZ):
    row, column = P(("dp", "tensor"), None), P(None, "tensor")
    return jax.shard_map(
        functools.partial(local, ny, nz),
        mesh=mesh,
        in_specs=(row, row, row, column, column, P("tensor", None)),
        out_specs=(row, row),
        check_vma=False,
    )
```

```python
import functools

import jax
import jax.numpy as jnp
from jax import lax
from jax.experimental import pallas as pl
from jax.experimental.pallas import tpu as pltpu
from jax.sharding import PartitionSpec as P

def firsts(n):
    return [2, -2, 1, -1] if n == 8 else [1, -1] if n == 4 else [1]


def seconds(n):
    return [2, -2] if n == 8 else []


def far_first(n):
    return sorted(range(1, n), key=lambda k: -min(k, n - k))


MESH = pl.DeviceIdType.MESH
f32, bf16 = jnp.float32, jnp.bfloat16
NT = (((1,), (1,)), ((), ()))
LANES = 128
PARTS = 4
NY, NZ, NC = 8, 4, 2


def kernel(
    ny, nz, xb, xa, xg, wg_hbm, wu_hbm, wd_hbm, out_b, out_a,
    wg, wu, wd, comm, commg, stage, op_t, op_g, part, psend, precv,
    s1, r1, t1, q1s, q1r, s2, r2, t2, q2s, q2r, w_sem, s_sem, r_sem,
):
    d = wg.shape[1]
    rows = d // LANES
    fine = rows // PARTS
    per_core = ny * nz
    tokens = per_core * NC

    t = lax.axis_index("tensor")
    c = lax.rem(t, NC)
    z = lax.rem(lax.div(t, NC), nz)
    y = lax.div(t, NC * nz)

    def at(yy, zz, cc):
        return {"tensor": (yy * nz + zz) * NC + cc}

    def yr(k):
        return lax.rem(y + k + ny, ny)

    def zr(k):
        return lax.rem(z + k + nz, nz)

    sib = at(y, z, 1 - c)
    sent = []

    def send(src, dst, dev):
        n = len(sent)
        cp = pltpu.make_async_remote_copy(
            src_ref=src, dst_ref=dst, send_sem=s_sem.at[n], recv_sem=r_sem.at[n], device_id=dev, device_id_type=MESH
        )
        cp.start()
        sent.append(cp)
        return cp

    loads = [
        pltpu.make_async_copy(h, v, w_sem.at[i])
        for i, (h, v) in enumerate(((wg_hbm, wg), (wu_hbm, wu), (wd_hbm, wd)))
    ]
    for cp in loads:
        cp.start()

    barrier = pltpu.get_barrier_semaphore()
    peers = [at(yr(k), z, c) for k in range(1, ny)] + [at(y, zr(k), c) for k in range(1, nz)] + [sib]
    for dev in peers:
        pl.semaphore_signal(barrier, inc=1, device_id=dev, device_id_type=MESH)

    def own_row(x, dst):
        for s in range(rows):
            stage[s : s + 1, :] = x[0:1, s * LANES : (s + 1) * LANES].astype(f32)
        dst[...] = stage[0:rows, :].astype(bf16)

    def place(k, n):
        return pl.ds(pl.multiple_of(k * n, n), n)

    own_row(xb, comm.at[c, y, place(2 * z, rows)])
    own_row(xa, comm.at[c, y, place(2 * z + 1, rows)])
    own_row(xg, commg.at[c, z, place(y, rows)])
    pl.semaphore_wait(barrier, len(peers))

    far_y, far_z = far_first(ny), far_first(nz)

    class Tokens:
        def __init__(self):
            self.along_z, self.near, self.far, self.shared = {}, {}, {}, {}

        def unit(self, ky, dz):
            return c, ky, place(zr(dz), 2 * rows)

        def go(self, ref, dev):
            return send(ref, ref, dev)

        def share(self, ky, dz):
            self.shared.setdefault(dz, []).append(self.go(comm.at[self.unit(ky, dz)], sib))

        def start(self):
            for k in far_z:
                self.along_z[k] = self.go(comm.at[self.unit(y, 0)], at(y, zr(k), c))

        def first(self, dz):
            if dz:
                self.along_z[(nz - dz) % nz].wait_recv()
            for k in firsts(ny):
                self.near[dz, k] = self.go(comm.at[self.unit(y, dz)], at(yr(k), z, c))
            self.share(y, dz)

        def second(self, dz):
            for k in seconds(ny):
                self.near[dz, k].wait_recv()
                one = place(2 * zr(dz) + (0 if k > 0 else 1), rows)
                self.far[dz, 2 * k] = self.go(comm.at[c, yr(-k), one], at(yr(k), z, c))
                self.far[dz, 3 * k // 2] = self.go(comm.at[self.unit(yr(-k), dz)], at(yr(k // 2), z, c))
                self.share(yr(-k), dz)

        def finish(self, dz):
            for k in firsts(ny):
                if k not in seconds(ny):
                    self.near[dz, k].wait_recv()
                    self.share(yr(-k), dz)
            for k in seconds(ny):
                self.far[dz, 3 * k // 2].wait_recv()
                self.share(yr(-3 * k // 2), dz)
            if seconds(ny):
                self.far[dz, 4].wait_recv()
                self.far[dz, -4].wait_recv()
                self.share(yr(4), dz)

        def to_operand(self):
            for dz, cps in self.shared.items():
                for cp in cps:
                    cp.wait_recv()
                for cc in range(NC):
                    for yy in range(ny):
                        for j in range(2):
                            lo = ((j * NC + cc) * ny + yy) * nz + zr(dz)
                            stage[place(lo, rows), :] = comm[cc, yy, place(2 * zr(dz) + j, rows)].astype(f32)
            to_operand(op_t, 2 * tokens)

    class Cotangents:
        def __init__(self):
            self.along_y, self.up, self.down, self.shared = [], [], [], []

        def piece(self, k, p):
            n = ny * rows // 2
            return commg.at[c, k, pl.ds(p * n, n)]

        def go(self, k, p, dz):
            ref = self.piece(k, p)
            return send(ref, ref, at(y, zr(dz), c))

        def share(self, k, p):
            ref = self.piece(k, p)
            self.shared.append(send(ref, ref, sib))

        def start(self):
            for k in far_y:
                ref = commg.at[c, z, place(y, rows)]
                self.along_y.append(send(ref, ref, at(yr(k), z, c)))

        def first(self):
            for cp in self.along_y:
                cp.wait_recv()
            for p in range(2):
                self.up.append(self.go(z, p, 1))
                self.down.append(self.go(z, 1 - p, -1))
            for p in range(2):
                self.share(z, p)

        def second(self):
            self.up[0].wait_recv()
            self.up.append(self.go(zr(-1), 0, 1))
            self.share(zr(-1), 0)
            self.down[0].wait_recv()
            self.down.append(self.go(zr(1), 1, -1))
            self.share(zr(1), 1)

        def finish(self):
            self.up[1].wait_recv()
            self.share(zr(-1), 1)
            self.down[1].wait_recv()
            self.share(zr(1), 0)
            self.up[2].wait_recv()
            self.share(zr(2), 0)
            self.down[2].wait_recv()
            self.share(zr(2), 1)

        def to_operand(self):
            for cp in self.shared:
                cp.wait_recv()
            for cc in range(NC):
                for zz in range(nz):
                    for yy in range(ny):
                        lo = ((cc * ny + yy) * nz + zz) * rows
                        stage[lo : lo + rows, :] = commg[cc, zz, yy * rows : (yy + 1) * rows].astype(f32)
            to_operand(op_g, tokens)

    def to_operand(op, n):
        for s in range(rows):
            op[:, s * LANES : (s + 1) * LANES] = stage[pl.ds(s, n, stride=rows), :].astype(bf16)

    def product(w, op):
        return lax.dot_general(op[...], w[...], NT, preferred_element_type=f32)

    width = d // PARTS
    core_rows = per_core * fine
    yb = nz * fine

    class Part:
        def __init__(self, i, q, pairs_of):
            self.at, self.buf, self.z_first = (i, q), (i, q // 2), q % 2 == 0
            v = sum(
                jnp.dot(left, w[:, q * width : (q + 1) * width], preferred_element_type=f32) for left, w in pairs_of
            )
            for s in range(fine):
                part[i, q, pl.ds(s, tokens, stride=fine), :] = v[:, s * LANES : (s + 1) * LANES]
            psend[i, q] = part[i, q, place(1 - c, core_rows), :].astype(bf16)
            self.pair = send(psend.at[i, q], precv.at[i, q], sib)

        def mine(self, lo, n):
            lo = pl.multiple_of(lo, n)
            own = part[(*self.at, pl.ds(pl.multiple_of(c * core_rows + lo, n), n))]
            return own + precv[(*self.at, pl.ds(lo, n))].astype(f32)

        def one(self):
            self.pair.wait_recv()
            self.cps = []
            b = self.buf
            if self.z_first:
                for k in far_z + [0]:
                    for yy in range(ny):
                        v = self.mine((yy * nz + zr(k)) * fine, fine)
                        if k:
                            s2[(*b, k - 1, slice(yy * fine, (yy + 1) * fine))] = v.astype(bf16)
                        else:
                            t2[(*b, slice(yy * fine, (yy + 1) * fine))] = v
                    if k:
                        self.cps.append(send(s2.at[(*b, k - 1)], r2.at[(*b, k - 1)], at(y, zr(k), c)))
            else:
                for k in far_y:
                    s1[(*b, k - 1)] = self.mine(yr(k) * yb, yb).astype(bf16)
                    self.cps.append(send(s1.at[(*b, k - 1)], r1.at[(*b, k - 1)], at(yr(k), z, c)))
                t1[b] = self.mine(y * yb, yb)

        def two(self):
            for cp in self.cps:
                cp.wait_recv()
            self.cps = []
            b = self.buf
            if self.z_first:
                v = t2[b]
                for k in range(nz - 1):
                    v = v + r2[(*b, k)].astype(f32)
                t2[b] = v
                for k in far_y:
                    q2s[(*b, k - 1)] = t2[(*b, place(yr(k), fine))].astype(bf16)
                    self.cps.append(send(q2s.at[(*b, k - 1)], q2r.at[(*b, k - 1)], at(yr(k), z, c)))
            else:
                v = t1[b]
                for k in range(ny - 1):
                    v = v + r1[(*b, k)].astype(f32)
                t1[b] = v
                for k in far_z:
                    q1s[(*b, k - 1)] = t1[(*b, place(zr(k), fine))].astype(bf16)
                    self.cps.append(send(q1s.at[(*b, k - 1)], q1r.at[(*b, k - 1)], at(y, zr(k), c)))

        def finish(self):
            for cp in self.cps:
                cp.wait_recv()
            b = self.buf
            if self.z_first:
                v = t2[(*b, place(y, fine))]
                for k in range(ny - 1):
                    v = v + q2r[(*b, k)].astype(f32)
            else:
                v = t1[(*b, place(z, fine))]
                for k in range(nz - 1):
                    v = v + q1r[(*b, k)].astype(f32)
            i, q = self.at
            (out_b, out_a)[i][q * fine : (q + 1) * fine, :] = v.astype(bf16)

    tt, tg = Tokens(), Cotangents()
    tt.start()
    tg.start()
    tt.first(0)
    tt.first(-1)
    tt.first(1)
    tt.first(2)
    tt.second(0)
    tg.first()
    tt.second(-1)
    tt.second(1)
    tg.second()
    tt.second(2)
    for dz in (0, -1, 1):
        tt.finish(dz)
    tg.finish()
    tt.finish(2)

    tt.to_operand()
    loads[0].wait()
    gate = product(wg, op_t)
    loads[1].wait()
    upper = product(wu, op_t)
    sigma = jax.nn.sigmoid(gate)
    hidden_b = (gate[:tokens] * sigma[:tokens] * upper[:tokens]).astype(bf16)
    gate, upper, sigma = gate[tokens:], upper[tokens:], sigma[tokens:]
    loads[2].wait()
    parts_b = [Part(0, q, [(hidden_b, wd)]) for q in range(PARTS)]
    parts_b[0].one()
    parts_b[1].one()
    tg.to_operand()
    parts_b[2].one()
    parts_b[3].one()
    grad_hidden = product(wd, op_g)
    grad_gate = (grad_hidden * upper * sigma * (1.0 + gate * (1.0 - sigma))).astype(bf16)
    grad_up = (grad_hidden * gate * sigma).astype(bf16)
    left_a = [(grad_gate, wg), (grad_up, wu)]
    parts_a = []
    for q in range(PARTS):
        parts_a.append(Part(1, q, left_a))
        if q:
            parts_a[q - 1].one()
    parts_a[-1].one()
    for p in parts_b + parts_a:
        p.two()
    for p in parts_b + parts_a:
        p.finish()
    for cp in sent:
        cp.wait_send()


def local(ny, nz, tokens_b, tokens_a, grad_out_a, gate_weight, up_weight, down_weight):
    h, d = down_weight.shape
    rows = d // LANES
    fine = rows // PARTS
    per_core = ny * nz
    tokens = per_core * NC
    vmem, dma = pltpu.VMEM, pltpu.SemaphoreType.DMA
    row = jax.ShapeDtypeStruct((rows, LANES), bf16)
    in_vmem, anywhere = pl.BlockSpec(memory_space=vmem), pl.BlockSpec(memory_space=pl.ANY)
    output_b, grad_in = pl.pallas_call(
        functools.partial(kernel, ny, nz),
        out_shape=(row, row),
        in_specs=[in_vmem] * 3 + [anywhere] * 3,
        out_specs=(in_vmem, in_vmem),
        scratch_shapes=[
            vmem((h, d), bf16),
            vmem((h, d), bf16),
            vmem((h, d), bf16),
            vmem((NC, ny, 2 * nz * rows, LANES), bf16),
            vmem((NC, nz, ny * rows, LANES), bf16),
            vmem((2 * tokens * rows, LANES), f32),
            vmem((2 * tokens, d), bf16),
            vmem((tokens, d), bf16),
            vmem((2, PARTS, tokens * fine, LANES), f32),
            vmem((2, PARTS, per_core * fine, LANES), bf16),
            vmem((2, PARTS, per_core * fine, LANES), bf16),
            vmem((2, 2, ny - 1, nz * fine, LANES), bf16),
            vmem((2, 2, ny - 1, nz * fine, LANES), bf16),
            vmem((2, 2, nz * fine, LANES), f32),
            vmem((2, 2, nz - 1, fine, LANES), bf16),
            vmem((2, 2, nz - 1, fine, LANES), bf16),
            vmem((2, 2, nz - 1, ny * fine, LANES), bf16),
            vmem((2, 2, nz - 1, ny * fine, LANES), bf16),
            vmem((2, 2, ny * fine, LANES), f32),
            vmem((2, 2, ny - 1, fine, LANES), bf16),
            vmem((2, 2, ny - 1, fine, LANES), bf16),
            dma((3,)),
            dma((192,)),
            dma((192,)),
        ],
        compiler_params=pltpu.CompilerParams(
            collective_id=0, has_side_effects=True, vmem_limit_bytes=60 * 2**20
        ),
        cost_estimate=pl.CostEstimate(flops=2 * 8 * tokens * d * h, bytes_accessed=6 * d * h, transcendentals=0),
        name="swiglu",
    )(tokens_b, tokens_a, grad_out_a, gate_weight.T, up_weight.T, down_weight)
    return output_b.reshape(1, d), grad_in.reshape(1, d)


def solution(mesh, ny=NY, nz=NZ):
    row, column = P(("dp", "tensor"), None), P(None, "tensor")
    return jax.shard_map(
        functools.partial(local, ny, nz),
        mesh=mesh,
        in_specs=(row, row, row, column, column, P("tensor", None)),
        out_specs=(row, row),
        check_vma=False,
    )
```
